32 devices in a mesh: pipe: 2 (over x), tensor: 4 (over z), dp: 4 (over y, core).
Axes of the slice: x: 2, y: 2, z: 4, core: 2. Of those that a mesh axis runs over, the one named last changes fastest.
Arguments:
- section_layers: int32 [2], replicated, may hold values from 9 to 11
- grad_out: bfloat16 [2, 4, 192, 4096], P('pipe', 'dp', 'tensor'), may hold values from -6 to 6
- gate_act: bfloat16 [2, 4, 192, 28672], P('pipe', 'dp', None, 'tensor'), may hold values from -6 to 6
- up_act: bfloat16 [2, 4, 192, 28672], P('pipe', 'dp', None, 'tensor'), may hold values from -6 to 6
- down_weight: bfloat16 [2, 28672, 4096], P('pipe', 'tensor'), may hold values from -0.09375 to 0.09375
Outputs:
- grad_gate: bfloat16 [2, 4, 192, 28672], P('pipe', 'dp', None, 'tensor')
- grad_up: bfloat16 [2, 4, 192, 28672], P('pipe', 'dp', None, 'tensor')
- grad_down_w: bfloat16 [2, 28672, 4096], P('pipe', ('tensor', 'dp'))
The draws below stay inside these ranges and needn't reach their ends.
All inputs are finite; a program needn't handle non-finite values.
Results may differ from the reference program's by a relative error of at most 0.013.
Values may be sent and summed in bfloat16 or wider, within the bound.
No kernel may reach another device: no remote copies, remote signals or barrier semaphores. Data moves between devices by JAX's collectives and lax.ppermute only.
A program may use at most 192 MiB of HBM per device.

```python
import jax
import jax.numpy as jnp
from jax import lax

D_WIN = 4096
FF = 28672
ROWS = 192
SECTIONS = 2
REPLICAS = 4


def draw_section_layers(key, part):
    fresh = jax.random.fold_in(jax.random.fold_in(key, 731), 4099)
    key_counts, key_high, key_step = jax.random.split(fresh, 3)
    counts = jax.random.randint(key_counts, (SECTIONS,), 9, 12).astype(jnp.int32)
    high_section = jax.random.randint(key_high, (), 0, SECTIONS).astype(jnp.int32)
    step_over = jax.random.randint(key_step, (), 1, SECTIONS).astype(jnp.int32)
    low_section = ((high_section + step_over) % SECTIONS).astype(jnp.int32)
    positions = jnp.arange(SECTIONS, dtype=jnp.int32)
    counts = jnp.where(positions == high_section, jnp.int32(11), counts)
    counts = jnp.where(positions == low_section, jnp.int32(9), counts)
    return counts.astype(jnp.int32)


def spiked(values, key, source, target, shards_of, factor):
    owner, partner = [(jnp.arange(values.shape[axis_at]) // (values.shape[axis_at] // shards_of)).reshape([-1 if axis == axis_at else 1 for axis in range(values.ndim)]) for axis_at in (source, target)]
    chosen = jax.random.permutation(key, shards_of)[partner]
    strong = (owner == chosen) | (owner == (partner + shards_of // 2) % shards_of)
    return jnp.where(strong, factor * values, values)


def level_of(own_key, shape, pieces, least, top_value):
    level, own = 1.0, jax.random.fold_in(own_key, 6)
    for dim, blocks in pieces:
        steps = jnp.exp(jax.random.uniform(jax.random.fold_in(own, dim), (blocks,), jnp.float32, least / len(pieces), top_value / len(pieces)))
        level = level * jnp.repeat(steps, shape[dim] // blocks).reshape([-1 if axis == dim else 1 for axis in range(len(shape))])
    return level


def normal_values(key, extent, width, bound, cuts=(), held_as=jnp.bfloat16):
    loudness = level_of(key, extent, cuts, -0.22, 0.18) if cuts else 1.0
    drawn = jax.random.normal(key, extent, jnp.float32) * width * loudness
    return jnp.minimum(jnp.maximum(drawn, -bound), bound).astype(held_as)


def heavy_noise(own_key, extent, spread, bound, shards, heavy, kind=jnp.bfloat16):
    array = spread * jax.random.normal(own_key, extent, jnp.float32)
    if shards:
        array = array * level_of(own_key, extent, shards, -0.22, 0.18)
    return jnp.clip(spiked(array, jax.random.fold_in(own_key, 3), *heavy), -bound, bound).astype(kind)


def setup_inputs(seed: int = 0) -> dict:
    key_of = jax.random.split(jax.random.key(seed), 6)
    section_layers = draw_section_layers(jax.random.fold_in(key_of[5], 71), 0)
    grad_out = normal_values(key_of[1], (SECTIONS, REPLICAS, ROWS, D_WIN), 1.0, 6.0, ((0, 2), (1, 4), (2, 4)))
    gate_act = normal_values(key_of[2], (SECTIONS, REPLICAS, ROWS, FF), 1.0, 6.0, ((0, 2), (1, 4), (3, 4)))
    up_act = heavy_noise(key_of[3], (SECTIONS, REPLICAS, ROWS, FF), 1.0, 6.0, ((0, 2), (1, 4), (3, 4)), (1, 3, 4, 2.0))
    down_weight = normal_values(key_of[4], (SECTIONS, FF, D_WIN), D_WIN ** -0.5, 0.09375, ((0, 2), (1, 4)))
    return {"section_layers": section_layers, "grad_out": grad_out, "gate_act": gate_act, "up_act": up_act, "down_weight": down_weight}


def one_section(inputs):
    scale, grad_rows, gate_in, up_in, weight = inputs
    gate = gate_in.astype(jnp.float32)
    up = up_in.astype(jnp.float32)
    logistic = jax.nn.sigmoid(gate)
    activated = gate * logistic
    hidden = (activated * up).astype(jnp.bfloat16)
    norm_scale = scale / jnp.sqrt(jnp.float32(ROWS * REPLICAS))

    def per_replica(running, items):
        rows_here, hidden_here = items
        grad_hidden = scale * lax.dot_general(rows_here, weight, (((1,), (1,)), ((), ())), preferred_element_type=jnp.float32)
        partial_sum = norm_scale * lax.dot_general(hidden_here, rows_here, (((0,), (0,)), ((), ())), preferred_element_type=jnp.float32)
        partial_sum = lax.optimization_barrier(partial_sum.astype(jnp.bfloat16))
        return (running + partial_sum.astype(jnp.float32), grad_hidden)
    start_sum = jnp.zeros((FF, D_WIN), jnp.float32)
    summed, grad_hidden = lax.scan(per_replica, start_sum, (grad_rows, hidden))
    grad_gate = (grad_hidden * up * logistic * (1.0 + gate * (1.0 - logistic))).astype(jnp.bfloat16)
    grad_up = (grad_hidden * activated).astype(jnp.bfloat16)
    return (grad_gate, grad_up, summed.astype(jnp.bfloat16))

def reference(section_layers, grad_out, gate_act, up_act, down_weight):
    offset = (jnp.cumsum(section_layers) - section_layers).astype(jnp.int32)
    scale = jnp.sqrt(10.0 / (offset + section_layers).astype(jnp.float32))
    grad_gate, grad_up, grad_down_w = lax.map(one_section, (scale, grad_out, gate_act, up_act, down_weight))
    return (grad_gate, grad_up, grad_down_w)
```

```python
import jax
import jax.numpy as jnp
from jax import lax
from jax.sharding import PartitionSpec as P


def section_scale(section_layers):
    section = lax.axis_index("pipe")
    positions = jnp.arange(section_layers.shape[0], dtype=jnp.int32)
    offset = jnp.sum(jnp.where(positions < section, section_layers, 0))
    layers_here = jnp.sum(jnp.where(positions == section, section_layers, 0))
    return jnp.sqrt(10.0 / (offset + layers_here).astype(jnp.float32))


def in_order(slots, place):
    count, rows = len(slots), slots[0].shape[0]
    whole = jnp.zeros((count * rows, slots[0].shape[1]), slots[0].dtype)
    for j, slot in enumerate(slots):
        block = lax.rem(place - j + count, count)
        whole = lax.dynamic_update_slice(whole, slot, (block * rows, 0))
    return whole


def per_device(section_layers, grad_out, gate_act, up_act, down_weight):
    scale = section_scale(section_layers)
    tensor, replicas = lax.axis_size("tensor"), lax.axis_size("dp")
    place, replica = lax.axis_index("tensor"), lax.axis_index("dp")
    own_rows = grad_out[0, 0]
    weight = down_weight[0]
    ring = [(i, (i + 1) % tensor) for i in range(tensor)]
    pair = [(i, i ^ 1) for i in range(replicas)]
    half = replicas // 2

    gate = gate_act[0, 0].astype(jnp.float32)
    up = up_act[0, 0].astype(jnp.float32)
    logistic = jax.nn.sigmoid(gate)
    activated = gate * logistic
    hidden = (activated * up).astype(jnp.bfloat16)
    rows, width = hidden.shape
    block = width // replicas

    def columns_of(owner, count=1):
        return lax.dynamic_slice(hidden, (0, owner * block), (rows, block * count))

    own_chip = replica // 2 * 2
    core = replica - own_chip
    row_parts, hidden_parts = [own_rows], []
    sent_hidden = []
    for step in range(1, half):
        to = [(i, (i + 2 * step) % replicas) for i in range(replicas)]
        row_parts.append(lax.ppermute(own_rows, "dp", to))
        sent_hidden.append(
            lax.ppermute(columns_of((own_chip + 2 * step) % replicas, 2), "dp", to)
        )
    mine, others = [columns_of(replica)], [columns_of(own_chip + 1 - core)]
    for pieces in sent_hidden:
        mine.append(lax.dynamic_slice(pieces, (0, core * block), (rows, block)))
        others.append(lax.dynamic_slice(pieces, (0, (1 - core) * block), (rows, block)))
    crossed = [lax.ppermute(piece, "dp", pair) for piece in others]

    gathered = []
    for part in row_parts:
        slots = [part]
        for _ in range(tensor - 1):
            slots.append(lax.ppermute(slots[-1], "tensor", ring))
        gathered.append(in_order(slots, place))
    all_rows = gathered[0]
    crossed_rows = [lax.ppermute(part, "dp", pair) for part in gathered]

    grad_hidden = scale * lax.dot_general(
        all_rows, weight, (((1,), (1,)), ((), ())), preferred_element_type=jnp.float32
    )
    grad_gate = (grad_hidden * up * logistic * (1.0 + gate * (1.0 - logistic))).astype(jnp.bfloat16)
    grad_up = (grad_hidden * activated).astype(jnp.bfloat16)

    norm_scale = scale / jnp.sqrt(jnp.float32(rows * replicas))
    every_hidden = jnp.concatenate(mine + crossed, axis=0)
    every_row = jnp.concatenate(gathered + crossed_rows, axis=0)
    summed = norm_scale * lax.dot_general(
        every_hidden, every_row, (((0,), (0,)), ((), ())), preferred_element_type=jnp.float32
    )
    grad_down_w = summed.astype(jnp.bfloat16)[None]
    return (grad_gate[None, None], grad_up[None, None], grad_down_w)


def solution(mesh):
    placed = (
        P(),
        P("pipe", "dp", "tensor", None),
        P("pipe", "dp", None, "tensor"),
        P("pipe", "dp", None, "tensor"),
        P("pipe", "tensor", None),
    )
    return jax.shard_map(
        per_device,
        mesh=mesh,
        in_specs=placed,
        out_specs=(
            P("pipe", "dp", None, "tensor"),
            P("pipe", "dp", None, "tensor"),
            P("pipe", ("tensor", "dp"), None),
        ),
        check_vma=False,
    )
```

```python
import functools

import jax
import jax.numpy as jnp
from jax import lax
from jax.experimental import pallas as pl
from jax.experimental.pallas import tpu as pltpu
from jax.sharding import PartitionSpec as P

VMEM_BYTES = 56 * 1024 * 1024
UNIT_STEP = 256
OUT_STEP = 512


def section_scale(section_layers):
    section = lax.axis_index("pipe")
    positions = jnp.arange(section_layers.shape[0], dtype=jnp.int32)
    offset = jnp.sum(jnp.where(positions < section, section_layers, 0))
    layers_here = jnp.sum(jnp.where(positions == section, section_layers, 0))
    return jnp.sqrt(10.0 / (offset + layers_here).astype(jnp.float32))


def after(value, *earlier):
    return lax.optimization_barrier((value, *earlier))[0]


def in_order(slots, place):
    count, rows = len(slots), slots[0].shape[0]
    whole = jnp.zeros((count * rows, slots[0].shape[1]), slots[0].dtype)
    for j, slot in enumerate(slots):
        block = lax.rem(place - j + count, count)
        whole = lax.dynamic_update_slice(whole, slot, (block * rows, 0))
    return whole


def general(section_layers, grad_out, gate_act, up_act, down_weight):
    scale = section_scale(section_layers)
    tensor, replicas = lax.axis_size("tensor"), lax.axis_size("dp")
    place, replica = lax.axis_index("tensor"), lax.axis_index("dp")
    own_rows = grad_out[0, 0]
    weight = down_weight[0]
    ring = [(i, (i + 1) % tensor) for i in range(tensor)]
    pair = [(i, i ^ 1) for i in range(replicas)]
    half = replicas // 2

    gate = gate_act[0, 0].astype(jnp.float32)
    up = up_act[0, 0].astype(jnp.float32)
    logistic = jax.nn.sigmoid(gate)
    activated = gate * logistic
    hidden = (activated * up).astype(jnp.bfloat16)
    rows, width = hidden.shape
    block = width // replicas

    def columns_of(owner, count=1):
        return lax.dynamic_slice(hidden, (0, owner * block), (rows, block * count))

    own_chip = replica // 2 * 2
    core = replica - own_chip
    row_parts, sent_hidden = [own_rows], []
    for step in range(1, half):
        to = [(i, (i + 2 * step) % replicas) for i in range(replicas)]
        row_parts.append(lax.ppermute(own_rows, "dp", to))
        sent_hidden.append(
            lax.ppermute(columns_of((own_chip + 2 * step) % replicas, 2), "dp", to)
        )
    mine, others = [columns_of(replica)], [columns_of(own_chip + 1 - core)]
    for pieces in sent_hidden:
        mine.append(lax.dynamic_slice(pieces, (0, core * block), (rows, block)))
        others.append(lax.dynamic_slice(pieces, (0, (1 - core) * block), (rows, block)))
    crossed = [lax.ppermute(piece, "dp", pair) for piece in others]

    gathered = []
    for part in row_parts:
        slots = [part]
        for _ in range(tensor - 1):
            slots.append(lax.ppermute(slots[-1], "tensor", ring))
        gathered.append(in_order(slots, place))
    all_rows = gathered[0]
    crossed_rows = [lax.ppermute(part, "dp", pair) for part in gathered]

    grad_hidden = scale * lax.dot_general(
        all_rows, weight, (((1,), (1,)), ((), ())), preferred_element_type=jnp.float32
    )
    grad_gate = (grad_hidden * up * logistic * (1.0 + gate * (1.0 - logistic))).astype(jnp.bfloat16)
    grad_up = (grad_hidden * activated).astype(jnp.bfloat16)

    norm_scale = scale / jnp.sqrt(jnp.float32(rows * replicas))
    every_hidden = jnp.concatenate(mine + crossed, axis=0)
    every_row = jnp.concatenate(gathered + crossed_rows, axis=0)
    summed = norm_scale * lax.dot_general(
        every_hidden, every_row, (((0,), (0,)), ((), ())), preferred_element_type=jnp.float32
    )
    return (grad_gate[None, None], grad_up[None, None], summed.astype(jnp.bfloat16)[None])


def factors_kernel(at, gate, up, hidden, gate_factor, up_factor):
    g, u = gate[...].astype(jnp.float32), up[...].astype(jnp.float32)
    logistic = 0.5 + 0.5 * jnp.tanh(0.5 * g)
    activated = g * logistic
    slope = logistic + activated * (1.0 - logistic)
    hidden[...] = (activated * u).astype(jnp.bfloat16)
    gate_factor[...] = (u * slope).astype(jnp.bfloat16)
    up_factor[...] = activated.astype(jnp.bfloat16)


def factors(at, gate, up, block, first):
    rows = gate.shape[0]
    half = block // 2
    out = jax.ShapeDtypeStruct((rows, block), jnp.bfloat16)
    spec = pl.BlockSpec(
        (rows, half), lambda i, at: (0, 2 * (at[first] if first >= 0 else -first - 1) + i)
    )
    return pl.pallas_call(
        factors_kernel,
        grid_spec=pltpu.PrefetchScalarGridSpec(
            num_scalar_prefetch=1,
            grid=(2,),
            in_specs=[spec, spec],
            out_specs=[pl.BlockSpec((rows, half), lambda i, at: (0, i))] * 3,
        ),
        out_shape=[out] * 3,
        compiler_params=pltpu.CompilerParams(vmem_limit_bytes=VMEM_BYTES),
        cost_estimate=pl.CostEstimate(flops=1000, bytes_accessed=1000, transcendentals=0),
        name="factors",
    )(at, gate, up)


def assemble_kernel(at, *refs):
    slots, whole = refs[:3], refs[3]
    piece, width = slots[0].shape[0], whole.shape[1]
    for j, slot in enumerate(slots):
        block = lax.rem(at[2] - j + 4, 4)
        there = pl.ds(pl.multiple_of(block * piece, piece), piece)
        whole[there, :] = slot[:, :width]


def assemble(at, slots, width):
    piece = slots[0].shape[0]
    return pl.pallas_call(
        assemble_kernel,
        grid_spec=pltpu.PrefetchScalarGridSpec(
            num_scalar_prefetch=1,
            grid=(1,),
            in_specs=[pl.BlockSpec((piece, width), lambda i, at: (0, 0))] * 3,
            out_specs=pl.BlockSpec((4 * piece, width), lambda i, at: (0, 0)),
        ),
        out_shape=jax.ShapeDtypeStruct((4 * piece, width), jnp.bfloat16),
        compiler_params=pltpu.CompilerParams(vmem_limit_bytes=VMEM_BYTES),
        cost_estimate=pl.CostEstimate(flops=1000, bytes_accessed=1000, transcendentals=0),
        name="assemble",
    )(at, *slots)


def complete_kernel(at, slot, earlier, whole):
    whole[...] = slot[...]


def complete(at, slot, whole):
    piece, width = slot.shape[0], whole.shape[1]
    return pl.pallas_call(
        complete_kernel,
        grid_spec=pltpu.PrefetchScalarGridSpec(
            num_scalar_prefetch=1,
            grid=(1,),
            in_specs=[
                pl.BlockSpec((piece, width), lambda i, at: (0, 0)),
                pl.BlockSpec(memory_space=pl.ANY),
            ],
            out_specs=pl.BlockSpec((piece, width), lambda i, at: (lax.rem(at[2] + 1, 4), 0)),
        ),
        out_shape=jax.ShapeDtypeStruct(whole.shape, jnp.bfloat16),
        input_output_aliases={2: 0},
        compiler_params=pltpu.CompilerParams(vmem_limit_bytes=VMEM_BYTES),
        cost_estimate=pl.CostEstimate(flops=1000, bytes_accessed=1000, transcendentals=0),
        name="complete",
    )(at, slot, whole)


def share_kernel(at, gate, up, gate_out, up_out):
    gate_out[...] = gate[...]
    up_out[...] = up[...]


def share(at, gate, up, block, first):
    rows = gate.shape[0]
    out = jax.ShapeDtypeStruct((rows, 2 * block), jnp.bfloat16)
    spec = pl.BlockSpec((rows, block), lambda i, at: (0, at[first + i]))
    return pl.pallas_call(
        share_kernel,
        grid_spec=pltpu.PrefetchScalarGridSpec(
            num_scalar_prefetch=1,
            grid=(2,),
            in_specs=[spec, spec],
            out_specs=[pl.BlockSpec((rows, block), lambda i, at: (0, i))] * 2,
        ),
        out_shape=[out] * 2,
        compiler_params=pltpu.CompilerParams(vmem_limit_bytes=VMEM_BYTES),
        cost_estimate=pl.CostEstimate(flops=1000, bytes_accessed=1000, transcendentals=0),
        name="share",
    )(at, gate, up)


def hidden_grad_kernel(at, scale, *refs):
    slots, weight = refs[:8], refs[8]
    own_mine, own_theirs, pair_mine, pair_theirs = refs[9:11], refs[11:13], refs[13:15], refs[15:17]
    own_out, pair_out = refs[17:19], refs[19:21]
    rows, product = refs[21:]
    chip, place = at[1], at[2]
    piece = slots[0].shape[0]
    count = 4 * piece

    @pl.when(pl.program_id(0) == 0)
    def _():
        for j in range(4):
            block = lax.rem(place - j + 4, 4)
            rows[pl.ds(pl.multiple_of(block * piece, piece), piece), :] = slots[j][...]
            there = pl.ds(pl.multiple_of(count + block * piece, piece), piece)
            rows[there, :] = slots[4 + j][...]

    units = weight.shape[2]
    both = weight[...].reshape(2 * units, weight.shape[3])
    part = lax.dot_general(
        rows[...], both, (((1,), (1,)), ((), ())), preferred_element_type=jnp.float32
    )
    product[0] = part[:, :units] * scale[0]
    product[1] = part[:, units:] * scale[0]
    for half, (own, pair) in enumerate(((own_mine, pair_mine), (own_theirs, pair_theirs))):
        here = product[chip if half == 0 else 1 - chip]
        for out, factor in zip(own_out, own):
            out[half] = (here[:count] * factor[...].astype(jnp.float32)).astype(jnp.bfloat16)
        for out, factor in zip(pair_out, pair):
            out[half] = (here[count:] * factor[...].astype(jnp.float32)).astype(jnp.bfloat16)


def hidden_grad(at, scale, slots, weight, factor_pairs, first, width):
    rows, block = factor_pairs[0][0].shape
    start = first // UNIT_STEP
    depth = weight.shape[1]
    halves = weight.reshape(2, 2, block, depth)
    factor_args = [value for pair in factor_pairs for value in pair]
    out = jax.ShapeDtypeStruct((2, rows, width), jnp.bfloat16)
    return pl.pallas_call(
        hidden_grad_kernel,
        grid_spec=pltpu.PrefetchScalarGridSpec(
            num_scalar_prefetch=1,
            grid=(width // UNIT_STEP,),
            in_specs=[pl.BlockSpec(memory_space=pltpu.SMEM)]
            + [pl.BlockSpec(slot.shape, lambda i, at: (0, 0)) for slot in slots]
            + [pl.BlockSpec((2, 1, UNIT_STEP, depth), lambda i, at: (0, at[0], start + i, 0))]
            + [pl.BlockSpec((rows, UNIT_STEP), lambda i, at: (0, start + i))] * 8,
            out_specs=[pl.BlockSpec((2, rows, UNIT_STEP), lambda i, at: (0, 0, i))] * 4
            + [pl.BlockSpec((2 * rows, depth), lambda i, at: (0, 0))],
            scratch_shapes=[pltpu.VMEM((2, 2 * rows, UNIT_STEP), jnp.float32)],
        ),
        out_shape=[out] * 4 + [jax.ShapeDtypeStruct((2 * rows, depth), jnp.bfloat16)],
        compiler_params=pltpu.CompilerParams(vmem_limit_bytes=VMEM_BYTES),
        cost_estimate=pl.CostEstimate(
            flops=1000,
            bytes_accessed=1000,
            transcendentals=0,
        ),
        name="hidden_grad",
    )(at, scale, *slots, halves, *factor_args)


def weight_grad_kernel(low_steps, at, norm, *refs):
    hidden, near, low, high = refs[:4], refs[4:6], refs[6:8], refs[8:16]
    own_new, wholes, out, held, every = refs[16:18], refs[18:20], refs[20], refs[21], refs[22]
    step = pl.program_id(0)
    count = hidden[0].shape[0]
    piece = count // 4

    @pl.when(step == 0)
    def _():
        for r in range(4):
            held[r * count : (r + 1) * count, :] = hidden[r][...]

    @pl.when(step < 2)
    def _():
        for whole, new in zip(wholes, own_new):
            whole[...] = new[0]

    for r in range(2):
        every[r * count : (r + 1) * count, :] = near[r][...]

    @pl.when(step < low_steps)
    def _():
        for r in range(2):
            every[(2 + r) * count : (3 + r) * count, :] = low[r][...]

    @pl.when(step >= low_steps)
    def _():
        for r in range(2):
            for j in range(4):
                block = lax.rem(at[2] - j + 4, 4)
                there = pl.ds(pl.multiple_of((2 + r) * count + block * piece, piece), piece)
                every[there, :] = high[4 * r + j][...]

    product = lax.dot_general(
        held[...], every[...], (((0,), (0,)), ((), ())), preferred_element_type=jnp.float32
    )
    out[...] = (product * norm[0]).astype(jnp.bfloat16)


def weight_grad(at, norm, hidden, rows, low, high, own_new):
    count, block = hidden[0].shape
    piece, depth = high[0].shape[0], rows.shape[1]
    low_steps = low[0].shape[1] // OUT_STEP
    specs = [pl.BlockSpec(memory_space=pltpu.SMEM)]
    specs += [pl.BlockSpec((count, block), lambda n, at: (0, 0))] * 4
    specs += [pl.BlockSpec((count, OUT_STEP), lambda n, at, r=r: (r, n)) for r in range(2)]
    specs += [pl.BlockSpec((count, OUT_STEP), lambda n, at: (0, jnp.minimum(n, low_steps - 1)))] * 2
    specs += [pl.BlockSpec((piece, OUT_STEP), lambda n, at: (0, jnp.maximum(n - low_steps, 0)))] * 8
    specs += [pl.BlockSpec((1, count, block), lambda n, at: (jnp.minimum(n, 1), 0, 0))] * 2
    whole = jax.ShapeDtypeStruct((count, 4 * block), jnp.bfloat16)
    return pl.pallas_call(
        functools.partial(weight_grad_kernel, low_steps),
        grid_spec=pltpu.PrefetchScalarGridSpec(
            num_scalar_prefetch=1,
            grid=(depth // OUT_STEP,),
            in_specs=specs,
            out_specs=[pl.BlockSpec((count, block), lambda n, at: (0, at[3 + jnp.minimum(n, 1)]))] * 2
            + [pl.BlockSpec((block, OUT_STEP), lambda n, at: (0, n))],
            scratch_shapes=[
                pltpu.VMEM((4 * count, block), jnp.bfloat16),
                pltpu.VMEM((4 * count, OUT_STEP), jnp.bfloat16),
            ],
        ),
        out_shape=[whole, whole, jax.ShapeDtypeStruct((block, depth), jnp.bfloat16)],
        compiler_params=pltpu.CompilerParams(vmem_limit_bytes=VMEM_BYTES),
        cost_estimate=pl.CostEstimate(flops=1000, bytes_accessed=1000, transcendentals=0),
        name="weight_grad",
    )(at, norm, *hidden, rows, rows, *low, *high, *own_new)


def place_kernel(at, gate, up, earlier_gate, earlier_up, gate_out, up_out):
    gate_out[...] = gate[...]
    up_out[...] = up[...]


def place_pair(at, news, wholes):
    count, block = news[0].shape[1:]
    return pl.pallas_call(
        place_kernel,
        grid_spec=pltpu.PrefetchScalarGridSpec(
            num_scalar_prefetch=1,
            grid=(2,),
            in_specs=[pl.BlockSpec((None, count, block), lambda n, at: (n, 0, 0))] * 2
            + [pl.BlockSpec(memory_space=pl.ANY)] * 2,
            out_specs=[pl.BlockSpec((count, block), lambda n, at: (0, at[5 + n]))] * 2,
        ),
        out_shape=[jax.ShapeDtypeStruct(whole.shape, whole.dtype) for whole in wholes],
        input_output_aliases={3: 0, 4: 1},
        compiler_params=pltpu.CompilerParams(vmem_limit_bytes=VMEM_BYTES),
        cost_estimate=pl.CostEstimate(flops=1000, bytes_accessed=1000, transcendentals=0),
        name="place_pair",
    )(at, *news, *wholes)


def paired(section_layers, grad_out, gate_act, up_act, down_weight):
    place, replica = lax.axis_index("tensor"), lax.axis_index("dp")
    chip, core = replica // 2, replica % 2
    across = [(0, 2), (1, 3), (2, 0), (3, 1)]
    pair = [(0, 1), (1, 0), (2, 3), (3, 2)]
    own_rows = grad_out[0, 0]
    gate, up, weight = gate_act[0, 0], up_act[0, 0], down_weight[0]
    rows, width = gate.shape
    depth = weight.shape[1]
    block = width // 4
    mine, theirs = 2 * chip + core, 2 * (1 - chip) + core
    pair_mine, pair_theirs = 2 * chip + 1 - core, 2 * (1 - chip) + 1 - core

    def to_pair(value):
        return lax.ppermute(value, "dp", pair)

    def to_across(value):
        return lax.ppermute(value, "dp", across)

    def around(value, places=1):
        return lax.ppermute(value, "tensor", [(i, (i + places) % 4) for i in range(4)])

    split = depth * 3 // 8 // OUT_STEP * OUT_STEP
    at = jnp.stack([core, chip, place, mine, theirs, pair_mine, pair_theirs]).astype(jnp.int32)
    slots = [own_rows, around(own_rows)]
    far_b0 = to_across(own_rows[:, split:])
    near = [to_pair(own_rows)]
    own_theirs = factors(at, gate, up, block, 4)
    shared = share(at, gate, up, block, 5)

    slots[1], far_b0, near[0], *shared, far_own = lax.optimization_barrier(
        (slots[1], far_b0, near[0], *shared, own_theirs[0])
    )
    slots.append(around(slots[1]))
    near.append(to_pair(slots[1]))
    pair_gate, pair_up = to_pair(shared[0]), to_pair(shared[1])
    far_own = to_across(far_own)
    pair_gate, pair_up, near[1] = lax.optimization_barrier((pair_gate, pair_up, near[1]))
    near_theirs = factors(at, pair_gate, pair_up, block, -2)
    near_mine = factors(at, pair_gate, pair_up, block, -1)

    slots[2], far_near, gate, section_layers, _ = lax.optimization_barrier(
        (slots[2], near_theirs[0], gate, section_layers, near_mine[0])
    )
    scale = section_scale(section_layers).reshape(1)
    norm = scale / jnp.sqrt(jnp.float32(rows * 4))
    slots.append(around(slots[2]))
    near.append(to_pair(slots[2]))
    cross_b = [to_pair(after(far_b0, slots[2]))]
    far_near = to_across(far_near)
    own_mine = factors(at, gate, up, block, 3)
    part = assemble(at, slots[:3], split)

    slots[3], near[2], cross_b[0], far_own, part, scale, norm, _ = lax.optimization_barrier(
        (slots[3], near[2], cross_b[0], far_own, part, scale, norm, own_mine[0])
    )
    near.append(to_pair(slots[3]))
    far_a = to_across(complete(at, slots[3], part))
    far_b = [far_b0] + [around(after(far_b0, slots[3]), places) for places in (1, 2, 3)]

    own_gate, own_up, near_gate, near_up, rows_here = hidden_grad(
        at, scale, [*slots, *near], weight,
        [own_mine[1:], own_theirs[1:], near_mine[1:], near_theirs[1:]], 0, block,
    )
    near_gate, near_up, far_near, far_a, *far_b = lax.optimization_barrier(
        (near_gate, near_up, far_near, far_a, *far_b)
    )
    cross_a = to_pair(far_a)
    cross_b += [to_pair(slot) for slot in far_b[1:]]
    near_gate, near_up, cross_a, *cross_b = lax.optimization_barrier(
        (near_gate, near_up, cross_a, *cross_b)
    )
    from_pair = [to_pair(near_gate), to_pair(near_up)]

    hidden = [own_mine[0], near_mine[0], far_own, far_near]
    grad_gate, grad_up, grad_down_w = weight_grad(
        at, norm, hidden, rows_here, [far_a, cross_a], [*far_b, *cross_b], [own_gate, own_up]
    )
    grad_gate, grad_up = place_pair(at, from_pair, [grad_gate, grad_up])
    return (grad_gate[None, None], grad_up[None, None], grad_down_w[None])


def solution(mesh):
    def per_device(section_layers, grad_out, gate_act, up_act, down_weight):
        sizes = (grad_out.shape[2] % 16, gate_act.shape[3] % 1024, grad_out.shape[3] % 1024)
        small = mesh.shape["tensor"] == 4 and mesh.shape["dp"] == 4
        form = paired if small and sizes == (0, 0, 0) else general
        return form(section_layers, grad_out, gate_act, up_act, down_weight)

    placed = (
        P(),
        P("pipe", "dp", "tensor", None),
        P("pipe", "dp", None, "tensor"),
        P("pipe", "dp", None, "tensor"),
        P("pipe", "tensor", None),
    )
    return jax.shard_map(
        per_device,
        mesh=mesh,
        in_specs=placed,
        out_specs=(
            P("pipe", "dp", None, "tensor"),
            P("pipe", "dp", None, "tensor"),
            P("pipe", ("tensor", "dp"), None),
        ),
        check_vma=False,
    )
```

```python
import functools

import jax
import jax.numpy as jnp
from jax import lax
from jax.experimental import pallas as pl
from jax.experimental.pallas import tpu as pltpu
from jax.sharding import PartitionSpec as P

VMEM_BYTES = 56 * 1024 * 1024
UNIT_STEP = 256
OUT_STEP = 512


def section_scale(section_layers):
    section = lax.axis_index("pipe")
    positions = jnp.arange(section_layers.shape[0], dtype=jnp.int32)
    offset = jnp.sum(jnp.where(positions < section, section_layers, 0))
    layers_here = jnp.sum(jnp.where(positions == section, section_layers, 0))
    return jnp.sqrt(10.0 / (offset + layers_here).astype(jnp.float32))


def after(value, *earlier):
    return lax.optimization_barrier((value, *earlier))[0]


def in_order(slots, place):
    count, rows = len(slots), slots[0].shape[0]
    whole = jnp.zeros((count * rows, slots[0].shape[1]), slots[0].dtype)
    for j, slot in enumerate(slots):
        block = lax.rem(place - j + count, count)
        whole = lax.dynamic_update_slice(whole, slot, (block * rows, 0))
    return whole


def general(section_layers, grad_out, gate_act, up_act, down_weight):
    scale = section_scale(section_layers)
    tensor, replicas = lax.axis_size("tensor"), lax.axis_size("dp")
    place, replica = lax.axis_index("tensor"), lax.axis_index("dp")
    own_rows = grad_out[0, 0]
    weight = down_weight[0]
    ring = [(i, (i + 1) % tensor) for i in range(tensor)]
    pair = [(i, i ^ 1) for i in range(replicas)]
    half = replicas // 2

    gate = gate_act[0, 0].astype(jnp.float32)
    up = up_act[0, 0].astype(jnp.float32)
    logistic = jax.nn.sigmoid(gate)
    activated = gate * logistic
    hidden = (activated * up).astype(jnp.bfloat16)
    rows, width = hidden.shape
    block = width // replicas

    def columns_of(owner, count=1):
        return lax.dynamic_slice(hidden, (0, owner * block), (rows, block * count))

    own_chip = replica // 2 * 2
    core = replica - own_chip
    row_parts, sent_hidden = [own_rows], []
    for step in range(1, half):
        to = [(i, (i + 2 * step) % replicas) for i in range(replicas)]
        row_parts.append(lax.ppermute(own_rows, "dp", to))
        sent_hidden.append(
            lax.ppermute(columns_of((own_chip + 2 * step) % replicas, 2), "dp", to)
        )
    mine, others = [columns_of(replica)], [columns_of(own_chip + 1 - core)]
    for pieces in sent_hidden:
        mine.append(lax.dynamic_slice(pieces, (0, core * block), (rows, block)))
        others.append(lax.dynamic_slice(pieces, (0, (1 - core) * block), (rows, block)))
    crossed = [lax.ppermute(piece, "dp", pair) for piece in others]

    gathered = []
    for part in row_parts:
        slots = [part]
        for _ in range(tensor - 1):
            slots.append(lax.ppermute(slots[-1], "tensor", ring))
        gathered.append(in_order(slots, place))
    all_rows = gathered[0]
    crossed_rows = [lax.ppermute(part, "dp", pair) for part in gathered]

    grad_hidden = scale * lax.dot_general(
        all_rows, weight, (((1,), (1,)), ((), ())), preferred_element_type=jnp.float32
    )
    grad_gate = (grad_hidden * up * logistic * (1.0 + gate * (1.0 - logistic))).astype(jnp.bfloat16)
    grad_up = (grad_hidden * activated).astype(jnp.bfloat16)

    norm_scale = scale / jnp.sqrt(jnp.float32(rows * replicas))
    every_hidden = jnp.concatenate(mine + crossed, axis=0)
    every_row = jnp.concatenate(gathered + crossed_rows, axis=0)
    summed = norm_scale * lax.dot_general(
        every_hidden, every_row, (((0,), (0,)), ((), ())), preferred_element_type=jnp.float32
    )
    return (grad_gate[None, None], grad_up[None, None], summed.astype(jnp.bfloat16)[None])


def factors_kernel(at, gate, up, hidden, gate_factor, up_factor):
    g, u = gate[...].astype(jnp.float32), up[...].astype(jnp.float32)
    logistic = 0.5 + 0.5 * jnp.tanh(0.5 * g)
    activated = g * logistic
    slope = logistic + activated * (1.0 - logistic)
    hidden[...] = (activated * u).astype(jnp.bfloat16)
    gate_factor[...] = (u * slope).astype(jnp.bfloat16)
    up_factor[...] = activated.astype(jnp.bfloat16)


def factors(at, gate, up, block, first):
    rows = gate.shape[0]
    half = block // 2
    out = jax.ShapeDtypeStruct((rows, block), jnp.bfloat16)
    spec = pl.BlockSpec(
        (rows, half), lambda i, at: (0, 2 * (at[first] if first >= 0 else -first - 1) + i)
    )
    return pl.pallas_call(
        factors_kernel,
        grid_spec=pltpu.PrefetchScalarGridSpec(
            num_scalar_prefetch=1,
            grid=(2,),
            in_specs=[spec, spec],
            out_specs=[pl.BlockSpec((rows, half), lambda i, at: (0, i))] * 3,
        ),
        out_shape=[out] * 3,
        compiler_params=pltpu.CompilerParams(vmem_limit_bytes=VMEM_BYTES),
        cost_estimate=pl.CostEstimate(flops=1000, bytes_accessed=1000, transcendentals=0),
        name="factors",
    )(at, gate, up)


def assemble_kernel(at, *refs):
    slots, whole = refs[:3], refs[3]
    piece, width = slots[0].shape[0], whole.shape[1]
    for j, slot in enumerate(slots):
        block = lax.rem(at[2] - j + 4, 4)
        there = pl.ds(pl.multiple_of(block * piece, piece), piece)
        whole[there, :] = slot[:, :width]


def assemble(at, slots, width):
    piece = slots[0].shape[0]
    return pl.pallas_call(
        assemble_kernel,
        grid_spec=pltpu.PrefetchScalarGridSpec(
            num_scalar_prefetch=1,
            grid=(1,),
            in_specs=[pl.BlockSpec((piece, width), lambda i, at: (0, 0))] * 3,
            out_specs=pl.BlockSpec((4 * piece, width), lambda i, at: (0, 0)),
        ),
        out_shape=jax.ShapeDtypeStruct((4 * piece, width), jnp.bfloat16),
        compiler_params=pltpu.CompilerParams(vmem_limit_bytes=VMEM_BYTES),
        cost_estimate=pl.CostEstimate(flops=1000, bytes_accessed=1000, transcendentals=0),
        name="assemble",
    )(at, *slots)


def share_kernel(at, gate, up, gate_out, up_out):
    gate_out[...] = gate[...]
    up_out[...] = up[...]


def share(at, gate, up, block, first):
    rows = gate.shape[0]
    out = jax.ShapeDtypeStruct((rows, 2 * block), jnp.bfloat16)
    spec = pl.BlockSpec((rows, block), lambda i, at: (0, at[first + i]))
    return pl.pallas_call(
        share_kernel,
        grid_spec=pltpu.PrefetchScalarGridSpec(
            num_scalar_prefetch=1,
            grid=(2,),
            in_specs=[spec, spec],
            out_specs=[pl.BlockSpec((rows, block), lambda i, at: (0, i))] * 2,
        ),
        out_shape=[out] * 2,
        compiler_params=pltpu.CompilerParams(vmem_limit_bytes=VMEM_BYTES),
        cost_estimate=pl.CostEstimate(flops=1000, bytes_accessed=1000, transcendentals=0),
        name="share",
    )(at, gate, up)


def hidden_grad_kernel(at, scale, *refs):
    slots, weight = refs[:8], refs[8]
    own_mine, own_theirs, pair_mine, pair_theirs = refs[9:11], refs[11:13], refs[13:15], refs[15:17]
    own_out, pair_out = refs[17:19], refs[19:21]
    rows, product = refs[21:]
    chip, place = at[1], at[2]
    piece = slots[0].shape[0]
    count = 4 * piece

    @pl.when(pl.program_id(0) == 0)
    def _():
        for j in range(4):
            block = lax.rem(place - j + 4, 4)
            rows[pl.ds(pl.multiple_of(block * piece, piece), piece), :] = slots[j][...]
            there = pl.ds(pl.multiple_of(count + block * piece, piece), piece)
            rows[there, :] = slots[4 + j][...]

    units = weight.shape[2]
    both = weight[...].reshape(2 * units, weight.shape[3])
    part = lax.dot_general(
        rows[...], both, (((1,), (1,)), ((), ())), preferred_element_type=jnp.float32
    )
    product[0] = part[:, :units] * scale[0]
    product[1] = part[:, units:] * scale[0]
    for half, (own, pair) in enumerate(((own_mine, pair_mine), (own_theirs, pair_theirs))):
        here = product[chip if half == 0 else 1 - chip]
        for out, factor in zip(own_out, own):
            out[half] = (here[:count] * factor[...].astype(jnp.float32)).astype(jnp.bfloat16)
        for out, factor in zip(pair_out, pair):
            out[half] = (here[count:] * factor[...].astype(jnp.float32)).astype(jnp.bfloat16)


def hidden_grad(at, scale, slots, weight, factor_pairs, first, width):
    rows, block = factor_pairs[0][0].shape
    start = first // UNIT_STEP
    depth = weight.shape[1]
    halves = weight.reshape(2, 2, block, depth)
    factor_args = [value for pair in factor_pairs for value in pair]
    out = jax.ShapeDtypeStruct((2, rows, width), jnp.bfloat16)
    return pl.pallas_call(
        hidden_grad_kernel,
        grid_spec=pltpu.PrefetchScalarGridSpec(
            num_scalar_prefetch=1,
            grid=(width // UNIT_STEP,),
            in_specs=[pl.BlockSpec(memory_space=pltpu.SMEM)]
            + [pl.BlockSpec(slot.shape, lambda i, at: (0, 0)) for slot in slots]
            + [pl.BlockSpec((2, 1, UNIT_STEP, depth), lambda i, at: (0, at[0], start + i, 0))]
            + [pl.BlockSpec((rows, UNIT_STEP), lambda i, at: (0, start + i))] * 8,
            out_specs=[pl.BlockSpec((2, rows, UNIT_STEP), lambda i, at: (0, 0, i))] * 4
            + [pl.BlockSpec((2 * rows, depth), lambda i, at: (0, 0))],
            scratch_shapes=[pltpu.VMEM((2, 2 * rows, UNIT_STEP), jnp.float32)],
        ),
        out_shape=[out] * 4 + [jax.ShapeDtypeStruct((2 * rows, depth), jnp.bfloat16)],
        compiler_params=pltpu.CompilerParams(vmem_limit_bytes=VMEM_BYTES),
        cost_estimate=pl.CostEstimate(
            flops=1000,
            bytes_accessed=1000,
            transcendentals=0,
        ),
        name="hidden_grad",
    )(at, scale, *slots, halves, *factor_args)


def weight_grad_kernel(low_steps, at, norm, *refs):
    hidden, near, low, high = refs[:4], refs[4:6], refs[6:8], refs[8:16]
    own_new, wholes, out, held, every = refs[16:18], refs[18:20], refs[20], refs[21], refs[22]
    step = pl.program_id(0)
    count = hidden[0].shape[0]
    piece = count // 4

    @pl.when(step == 0)
    def _():
        for r in range(4):
            held[r * count : (r + 1) * count, :] = hidden[r][...]

    @pl.when(step < 2)
    def _():
        for whole, new in zip(wholes, own_new):
            whole[...] = new[0]

    for r in range(2):
        every[r * count : (r + 1) * count, :] = near[r][...]

    @pl.when(step < low_steps)
    def _():
        for r in range(2):
            every[(2 + r) * count : (3 + r) * count, :] = low[r][...]

    @pl.when(step >= low_steps)
    def _():
        for r in range(2):
            for j in range(4):
                block = lax.rem(at[2] - j + 4, 4)
                there = pl.ds(pl.multiple_of((2 + r) * count + block * piece, piece), piece)
                every[there, :] = high[4 * r + j][...]

    product = lax.dot_general(
        held[...], every[...], (((0,), (0,)), ((), ())), preferred_element_type=jnp.float32
    )
    out[...] = (product * norm[0]).astype(jnp.bfloat16)


def weight_grad(at, norm, hidden, rows, low, high, own_new):
    count, block = hidden[0].shape
    piece, depth = high[0].shape[0], rows.shape[1]
    low_steps = low[0].shape[1] // OUT_STEP
    specs = [pl.BlockSpec(memory_space=pltpu.SMEM)]
    specs += [pl.BlockSpec((count, block), lambda n, at: (0, 0))] * 4
    specs += [pl.BlockSpec((count, OUT_STEP), lambda n, at, r=r: (r, n)) for r in range(2)]
    specs += [pl.BlockSpec((count, OUT_STEP), lambda n, at: (0, jnp.minimum(n, low_steps - 1)))] * 2
    specs += [pl.BlockSpec((piece, OUT_STEP), lambda n, at: (0, jnp.maximum(n - low_steps, 0)))] * 8
    specs += [pl.BlockSpec((1, count, block), lambda n, at: (jnp.minimum(n, 1), 0, 0))] * 2
    whole = jax.ShapeDtypeStruct((count, 4 * block), jnp.bfloat16)
    return pl.pallas_call(
        functools.partial(weight_grad_kernel, low_steps),
        grid_spec=pltpu.PrefetchScalarGridSpec(
            num_scalar_prefetch=1,
            grid=(depth // OUT_STEP,),
            in_specs=specs,
            out_specs=[pl.BlockSpec((count, block), lambda n, at: (0, at[3 + jnp.minimum(n, 1)]))] * 2
            + [pl.BlockSpec((block, OUT_STEP), lambda n, at: (0, n))],
            scratch_shapes=[
                pltpu.VMEM((4 * count, block), jnp.bfloat16),
                pltpu.VMEM((4 * count, OUT_STEP), jnp.bfloat16),
            ],
        ),
        out_shape=[whole, whole, jax.ShapeDtypeStruct((block, depth), jnp.bfloat16)],
        compiler_params=pltpu.CompilerParams(vmem_limit_bytes=VMEM_BYTES),
        cost_estimate=pl.CostEstimate(flops=1000, bytes_accessed=1000, transcendentals=0),
        name="weight_grad",
    )(at, norm, *hidden, rows, rows, *low, *high, *own_new)


def paired(section_layers, grad_out, gate_act, up_act, down_weight):
    place, replica = lax.axis_index("tensor"), lax.axis_index("dp")
    chip, core = replica // 2, replica % 2
    across = [(0, 2), (1, 3), (2, 0), (3, 1)]
    pair = [(0, 1), (1, 0), (2, 3), (3, 2)]
    own_rows = grad_out[0, 0]
    gate, up, weight = gate_act[0, 0], up_act[0, 0], down_weight[0]
    rows, width = gate.shape
    depth = weight.shape[1]
    block = width // 4
    mine, theirs = 2 * chip + core, 2 * (1 - chip) + core
    pair_mine, pair_theirs = 2 * chip + 1 - core, 2 * (1 - chip) + 1 - core

    def to_pair(value):
        return lax.ppermute(value, "dp", pair)

    def to_across(value):
        return lax.ppermute(value, "dp", across)

    def around(value, places=1):
        return lax.ppermute(value, "tensor", [(i, (i + places) % 4) for i in range(4)])

    split = depth * 3 // 8 // OUT_STEP * OUT_STEP
    at = jnp.stack([core, chip, place, mine, theirs, pair_mine, pair_theirs]).astype(jnp.int32)
    slots = [own_rows, around(own_rows)]
    far_b0 = to_across(own_rows[:, split:])
    near = [to_pair(own_rows)]
    own_theirs = factors(at, gate, up, block, 4)
    shared = share(at, gate, up, block, 5)

    slots[1], far_b0, near[0], *shared, far_own = lax.optimization_barrier(
        (slots[1], far_b0, near[0], *shared, own_theirs[0])
    )
    slots.append(around(slots[1]))
    near.append(to_pair(slots[1]))
    pair_gate, pair_up = to_pair(shared[0]), to_pair(shared[1])
    far_own = to_across(far_own)
    pair_gate, pair_up, near[1] = lax.optimization_barrier((pair_gate, pair_up, near[1]))
    near_theirs = factors(at, pair_gate, pair_up, block, -2)

    slots[2], far_near, gate, pair_gate, section_layers = lax.optimization_barrier(
        (slots[2], near_theirs[0], gate, pair_gate, section_layers)
    )
    scale = section_scale(section_layers).reshape(1)
    norm = scale / jnp.sqrt(jnp.float32(rows * 4))
    slots.append(around(slots[2]))
    near.append(to_pair(slots[2]))
    cross_b = [to_pair(after(far_b0, slots[2]))]
    far_near = to_across(far_near)
    own_mine = factors(at, gate, up, block, 3)
    near_mine = factors(at, pair_gate, pair_up, block, -1)
    part = assemble(at, slots[:3], split)

    slots[3], near[2], cross_b[0], far_own, part, scale, norm, _, _ = lax.optimization_barrier(
        (slots[3], near[2], cross_b[0], far_own, part, scale, norm, own_mine[0], near_mine[0])
    )
    near.append(to_pair(slots[3]))
    piece = slots[3].shape[0]
    part = lax.dynamic_update_slice(part, slots[3][:, :split], (lax.rem(place + 1, 4) * piece, 0))
    far_a = to_across(part)
    far_b = [far_b0] + [around(after(far_b0, slots[3]), places) for places in (1, 2, 3)]

    own_gate, own_up, near_gate, near_up, rows_here = hidden_grad(
        at, scale, [*slots, *near], weight,
        [own_mine[1:], own_theirs[1:], near_mine[1:], near_theirs[1:]], 0, block,
    )
    near_gate, near_up, far_near, far_a, *far_b = lax.optimization_barrier(
        (near_gate, near_up, far_near, far_a, *far_b)
    )
    cross_a = to_pair(far_a)
    cross_b += [to_pair(slot) for slot in far_b[1:]]
    near_gate, near_up, cross_a, *cross_b = lax.optimization_barrier(
        (near_gate, near_up, cross_a, *cross_b)
    )
    from_pair = [to_pair(near_gate), to_pair(near_up)]

    hidden = [own_mine[0], near_mine[0], far_own, far_near]
    grad_gate, grad_up, grad_down_w = weight_grad(
        at, norm, hidden, rows_here, [far_a, cross_a], [*far_b, *cross_b], [own_gate, own_up]
    )
    for i, owner in enumerate((pair_mine, pair_theirs)):
        grad_gate = lax.dynamic_update_slice(grad_gate, from_pair[0][i], (0, owner * block))
        grad_up = lax.dynamic_update_slice(grad_up, from_pair[1][i], (0, owner * block))
    return (grad_gate[None, None], grad_up[None, None], grad_down_w[None])


def solution(mesh):
    def per_device(section_layers, grad_out, gate_act, up_act, down_weight):
        sizes = (grad_out.shape[2] % 16, gate_act.shape[3] % 1024, grad_out.shape[3] % 1024)
        small = mesh.shape["tensor"] == 4 and mesh.shape["dp"] == 4
        form = paired if small and sizes == (0, 0, 0) else general
        return form(section_layers, grad_out, gate_act, up_act, down_weight)

    placed = (
        P(),
        P("pipe", "dp", "tensor", None),
        P("pipe", "dp", None, "tensor"),
        P("pipe", "dp", None, "tensor"),
        P("pipe", "tensor", None),
    )
    return jax.shard_map(
        per_device,
        mesh=mesh,
        in_specs=placed,
        out_specs=(
            P("pipe", "dp", None, "tensor"),
            P("pipe", "dp", None, "tensor"),
            P("pipe", ("tensor", "dp"), None),
        ),
        check_vma=False,
    )
```

```python
import functools

import jax
import jax.numpy as jnp
from jax import lax
from jax.experimental import pallas as pl
from jax.experimental.pallas import tpu as pltpu
from jax.sharding import PartitionSpec as P

VMEM_BYTES = 56 * 1024 * 1024
UNIT_STEP = 256
OUT_STEP = 512


def section_scale(section_layers):
    section = lax.axis_index("pipe")
    positions = jnp.arange(section_layers.shape[0], dtype=jnp.int32)
    offset = jnp.sum(jnp.where(positions < section, section_layers, 0))
    layers_here = jnp.sum(jnp.where(positions == section, section_layers, 0))
    return jnp.sqrt(10.0 / (offset + layers_here).astype(jnp.float32))


def after(value, *earlier):
    return lax.optimization_barrier((value, *earlier))[0]


def in_order(slots, place):
    count, rows = len(slots), slots[0].shape[0]
    whole = jnp.zeros((count * rows, slots[0].shape[1]), slots[0].dtype)
    for j, slot in enumerate(slots):
        block = lax.rem(place - j + count, count)
        whole = lax.dynamic_update_slice(whole, slot, (block * rows, 0))
    return whole


def general(section_layers, grad_out, gate_act, up_act, down_weight):
    scale = section_scale(section_layers)
    tensor, replicas = lax.axis_size("tensor"), lax.axis_size("dp")
    place, replica = lax.axis_index("tensor"), lax.axis_index("dp")
    own_rows = grad_out[0, 0]
    weight = down_weight[0]
    ring = [(i, (i + 1) % tensor) for i in range(tensor)]
    pair = [(i, i ^ 1) for i in range(replicas)]
    half = replicas // 2

    gate = gate_act[0, 0].astype(jnp.float32)
    up = up_act[0, 0].astype(jnp.float32)
    logistic = jax.nn.sigmoid(gate)
    activated = gate * logistic
    hidden = (activated * up).astype(jnp.bfloat16)
    rows, width = hidden.shape
    block = width // replicas

    def columns_of(owner, count=1):
        return lax.dynamic_slice(hidden, (0, owner * block), (rows, block * count))

    own_chip = replica // 2 * 2
    core = replica - own_chip
    row_parts, sent_hidden = [own_rows], []
    for step in range(1, half):
        to = [(i, (i + 2 * step) % replicas) for i in range(replicas)]
        row_parts.append(lax.ppermute(own_rows, "dp", to))
        sent_hidden.append(
            lax.ppermute(columns_of((own_chip + 2 * step) % replicas, 2), "dp", to)
        )
    mine, others = [columns_of(replica)], [columns_of(own_chip + 1 - core)]
    for pieces in sent_hidden:
        mine.append(lax.dynamic_slice(pieces, (0, core * block), (rows, block)))
        others.append(lax.dynamic_slice(pieces, (0, (1 - core) * block), (rows, block)))
    crossed = [lax.ppermute(piece, "dp", pair) for piece in others]

    gathered = []
    for part in row_parts:
        slots = [part]
        for _ in range(tensor - 1):
            slots.append(lax.ppermute(slots[-1], "tensor", ring))
        gathered.append(in_order(slots, place))
    all_rows = gathered[0]
    crossed_rows = [lax.ppermute(part, "dp", pair) for part in gathered]

    grad_hidden = scale * lax.dot_general(
        all_rows, weight, (((1,), (1,)), ((), ())), preferred_element_type=jnp.float32
    )
    grad_gate = (grad_hidden * up * logistic * (1.0 + gate * (1.0 - logistic))).astype(jnp.bfloat16)
    grad_up = (grad_hidden * activated).astype(jnp.bfloat16)

    norm_scale = scale / jnp.sqrt(jnp.float32(rows * replicas))
    every_hidden = jnp.concatenate(mine + crossed, axis=0)
    every_row = jnp.concatenate(gathered + crossed_rows, axis=0)
    summed = norm_scale * lax.dot_general(
        every_hidden, every_row, (((0,), (0,)), ((), ())), preferred_element_type=jnp.float32
    )
    return (grad_gate[None, None], grad_up[None, None], summed.astype(jnp.bfloat16)[None])


def factors_kernel(at, gate, up, hidden, gate_factor, up_factor):
    g, u = gate[...].astype(jnp.float32), up[...].astype(jnp.float32)
    logistic = 0.5 + 0.5 * jnp.tanh(0.5 * g)
    activated = g * logistic
    slope = logistic + activated * (1.0 - logistic)
    hidden[...] = (activated * u).astype(jnp.bfloat16)
    gate_factor[...] = (u * slope).astype(jnp.bfloat16)
    up_factor[...] = activated.astype(jnp.bfloat16)


def factors(at, gate, up, block, first):
    rows = gate.shape[0]
    half = block // 2
    out = jax.ShapeDtypeStruct((rows, block), jnp.bfloat16)
    spec = pl.BlockSpec(
        (rows, half), lambda i, at: (0, 2 * (at[first] if first >= 0 else -first - 1) + i)
    )
    return pl.pallas_call(
        factors_kernel,
        grid_spec=pltpu.PrefetchScalarGridSpec(
            num_scalar_prefetch=1,
            grid=(2,),
            in_specs=[spec, spec],
            out_specs=[pl.BlockSpec((rows, half), lambda i, at: (0, i))] * 3,
        ),
        out_shape=[out] * 3,
        compiler_params=pltpu.CompilerParams(vmem_limit_bytes=VMEM_BYTES),
        cost_estimate=pl.CostEstimate(flops=1000, bytes_accessed=1000, transcendentals=0),
        name="factors",
    )(at, gate, up)


def assemble_kernel(at, *refs):
    slots, whole = refs[:3], refs[3]
    piece, width = slots[0].shape[0], whole.shape[1]
    for j, slot in enumerate(slots):
        block = lax.rem(at[2] - j + 4, 4)
        there = pl.ds(pl.multiple_of(block * piece, piece), piece)
        whole[there, :] = slot[:, :width]


def assemble(at, slots, width):
    piece = slots[0].shape[0]
    return pl.pallas_call(
        assemble_kernel,
        grid_spec=pltpu.PrefetchScalarGridSpec(
            num_scalar_prefetch=1,
            grid=(1,),
            in_specs=[pl.BlockSpec((piece, width), lambda i, at: (0, 0))] * 3,
            out_specs=pl.BlockSpec((4 * piece, width), lambda i, at: (0, 0)),
        ),
        out_shape=jax.ShapeDtypeStruct((4 * piece, width), jnp.bfloat16),
        compiler_params=pltpu.CompilerParams(vmem_limit_bytes=VMEM_BYTES),
        cost_estimate=pl.CostEstimate(flops=1000, bytes_accessed=1000, transcendentals=0),
        name="assemble",
    )(at, *slots)


def share_kernel(at, gate, up, gate_out, up_out):
    gate_out[...] = gate[...]
    up_out[...] = up[...]


def share(at, gate, up, block, first):
    rows = gate.shape[0]
    out = jax.ShapeDtypeStruct((rows, 2 * block), jnp.bfloat16)
    spec = pl.BlockSpec((rows, block), lambda i, at: (0, at[first + i]))
    return pl.pallas_call(
        share_kernel,
        grid_spec=pltpu.PrefetchScalarGridSpec(
            num_scalar_prefetch=1,
            grid=(2,),
            in_specs=[spec, spec],
            out_specs=[pl.BlockSpec((rows, block), lambda i, at: (0, i))] * 2,
        ),
        out_shape=[out] * 2,
        compiler_params=pltpu.CompilerParams(vmem_limit_bytes=VMEM_BYTES),
        cost_estimate=pl.CostEstimate(flops=1000, bytes_accessed=1000, transcendentals=0),
        name="share",
    )(at, gate, up)


def hidden_grad_kernel(at, scale, *refs):
    slots, weight = refs[:8], refs[8]
    own_mine, own_theirs, pair_mine, pair_theirs = refs[9:11], refs[11:13], refs[13:15], refs[15:17]
    own_out, pair_out = refs[17:19], refs[19:21]
    rows_out, product, rows, sem = refs[21:]
    copy_out = pltpu.make_async_copy(rows, rows_out, sem)
    chip, place = at[1], at[2]
    piece = slots[0].shape[0]
    count = 4 * piece

    @pl.when(pl.program_id(0) == 0)
    def _():
        for j in range(4):
            block = lax.rem(place - j + 4, 4)
            rows[pl.ds(pl.multiple_of(block * piece, piece), piece), :] = slots[j][...]
            there = pl.ds(pl.multiple_of(count + block * piece, piece), piece)
            rows[there, :] = slots[4 + j][...]
        copy_out.start()

    units = weight.shape[2]
    both = weight[...].reshape(2 * units, weight.shape[3])
    part = lax.dot_general(
        rows[...], both, (((1,), (1,)), ((), ())), preferred_element_type=jnp.float32
    )
    product[0] = part[:, :units] * scale[0]
    product[1] = part[:, units:] * scale[0]
    for half, (own, pair) in enumerate(((own_mine, pair_mine), (own_theirs, pair_theirs))):
        here = product[chip if half == 0 else 1 - chip]
        for out, factor in zip(own_out, own):
            out[half] = (here[:count] * factor[...].astype(jnp.float32)).astype(jnp.bfloat16)
        for out, factor in zip(pair_out, pair):
            out[half] = (here[count:] * factor[...].astype(jnp.float32)).astype(jnp.bfloat16)

    @pl.when(pl.program_id(0) == pl.num_programs(0) - 1)
    def _():
        copy_out.wait()


def hidden_grad(at, scale, slots, weight, factor_pairs, first, width):
    rows, block = factor_pairs[0][0].shape
    start = first // UNIT_STEP
    depth = weight.shape[1]
    halves = weight.reshape(2, 2, block, depth)
    factor_args = [value for pair in factor_pairs for value in pair]
    out = jax.ShapeDtypeStruct((2, rows, width), jnp.bfloat16)
    return pl.pallas_call(
        hidden_grad_kernel,
        grid_spec=pltpu.PrefetchScalarGridSpec(
            num_scalar_prefetch=1,
            grid=(width // UNIT_STEP,),
            in_specs=[pl.BlockSpec(memory_space=pltpu.SMEM)]
            + [pl.BlockSpec(slot.shape, lambda i, at: (0, 0)) for slot in slots]
            + [pl.BlockSpec((2, 1, UNIT_STEP, depth), lambda i, at: (0, at[0], start + i, 0))]
            + [pl.BlockSpec((rows, UNIT_STEP), lambda i, at: (0, start + i))] * 8,
            out_specs=[pl.BlockSpec((2, rows, UNIT_STEP), lambda i, at: (0, 0, i))] * 4
            + [pl.BlockSpec(memory_space=pl.ANY)],
            scratch_shapes=[
                pltpu.VMEM((2, 2 * rows, UNIT_STEP), jnp.float32),
                pltpu.VMEM((2 * rows, depth), jnp.bfloat16),
                pltpu.SemaphoreType.DMA,
            ],
        ),
        out_shape=[out] * 4 + [jax.ShapeDtypeStruct((2 * rows, depth), jnp.bfloat16)],
        compiler_params=pltpu.CompilerParams(vmem_limit_bytes=VMEM_BYTES),
        cost_estimate=pl.CostEstimate(
            flops=1000,
            bytes_accessed=1000,
            transcendentals=0,
        ),
        name="hidden_grad",
    )(at, scale, *slots, halves, *factor_args)


def weight_grad_kernel(low_steps, at, norm, *refs):
    hidden, near, low, high = refs[:4], refs[4:6], refs[6:8], refs[8:16]
    own_new, wholes, out, held, every = refs[16:18], refs[18:20], refs[20], refs[21], refs[22]
    step = pl.program_id(0)
    count = hidden[0].shape[0]
    piece = count // 4

    @pl.when(step == 0)
    def _():
        for r in range(4):
            held[r * count : (r + 1) * count, :] = hidden[r][...]

    @pl.when(step < 2)
    def _():
        for whole, new in zip(wholes, own_new):
            whole[...] = new[0]

    for r in range(2):
        every[r * count : (r + 1) * count, :] = near[r][...]

    @pl.when(step < low_steps)
    def _():
        for r in range(2):
            every[(2 + r) * count : (3 + r) * count, :] = low[r][...]

    @pl.when(step >= low_steps)
    def _():
        for r in range(2):
            for j in range(4):
                block = lax.rem(at[2] - j + 4, 4)
                there = pl.ds(pl.multiple_of((2 + r) * count + block * piece, piece), piece)
                every[there, :] = high[4 * r + j][...]

    product = lax.dot_general(
        held[...], every[...], (((0,), (0,)), ((), ())), preferred_element_type=jnp.float32
    )
    out[...] = (product * norm[0]).astype(jnp.bfloat16)


def weight_grad(at, norm, hidden, rows, low, high, own_new):
    count, block = hidden[0].shape
    piece, depth = high[0].shape[0], rows.shape[1]
    low_steps = low[0].shape[1] // OUT_STEP
    specs = [pl.BlockSpec(memory_space=pltpu.SMEM)]
    specs += [pl.BlockSpec((count, block), lambda n, at: (0, 0))] * 4
    specs += [pl.BlockSpec((count, OUT_STEP), lambda n, at, r=r: (r, n)) for r in range(2)]
    specs += [pl.BlockSpec((count, OUT_STEP), lambda n, at: (0, jnp.minimum(n, low_steps - 1)))] * 2
    specs += [pl.BlockSpec((piece, OUT_STEP), lambda n, at: (0, jnp.maximum(n - low_steps, 0)))] * 8
    specs += [pl.BlockSpec((1, count, block), lambda n, at: (jnp.minimum(n, 1), 0, 0))] * 2
    whole = jax.ShapeDtypeStruct((count, 4 * block), jnp.bfloat16)
    return pl.pallas_call(
        functools.partial(weight_grad_kernel, low_steps),
        grid_spec=pltpu.PrefetchScalarGridSpec(
            num_scalar_prefetch=1,
            grid=(depth // OUT_STEP,),
            in_specs=specs,
            out_specs=[pl.BlockSpec((count, block), lambda n, at: (0, at[3 + jnp.minimum(n, 1)]))] * 2
            + [pl.BlockSpec((block, OUT_STEP), lambda n, at: (0, n))],
            scratch_shapes=[
                pltpu.VMEM((4 * count, block), jnp.bfloat16),
                pltpu.VMEM((4 * count, OUT_STEP), jnp.bfloat16),
            ],
        ),
        out_shape=[whole, whole, jax.ShapeDtypeStruct((block, depth), jnp.bfloat16)],
        compiler_params=pltpu.CompilerParams(vmem_limit_bytes=VMEM_BYTES),
        cost_estimate=pl.CostEstimate(flops=1000, bytes_accessed=1000, transcendentals=0),
        name="weight_grad",
    )(at, norm, *hidden, rows, rows, *low, *high, *own_new)


def paired(section_layers, grad_out, gate_act, up_act, down_weight):
    place, replica = lax.axis_index("tensor"), lax.axis_index("dp")
    chip, core = replica // 2, replica % 2
    across = [(0, 2), (1, 3), (2, 0), (3, 1)]
    pair = [(0, 1), (1, 0), (2, 3), (3, 2)]
    own_rows = grad_out[0, 0]
    gate, up, weight = gate_act[0, 0], up_act[0, 0], down_weight[0]
    rows, width = gate.shape
    depth = weight.shape[1]
    block = width // 4
    mine, theirs = 2 * chip + core, 2 * (1 - chip) + core
    pair_mine, pair_theirs = 2 * chip + 1 - core, 2 * (1 - chip) + 1 - core

    def to_pair(value):
        return lax.ppermute(value, "dp", pair)

    def to_across(value):
        return lax.ppermute(value, "dp", across)

    def around(value, places=1):
        return lax.ppermute(value, "tensor", [(i, (i + places) % 4) for i in range(4)])

    split = depth * 3 // 8 // OUT_STEP * OUT_STEP
    at = jnp.stack([core, chip, place, mine, theirs, pair_mine, pair_theirs]).astype(jnp.int32)
    slots = [own_rows, around(own_rows)]
    far_b0 = to_across(own_rows[:, split:])
    near = [to_pair(own_rows)]
    own_theirs = factors(at, gate, up, block, 4)
    shared = share(at, gate, up, block, 5)

    slots[1], far_b0, near[0], *shared, far_own = lax.optimization_barrier(
        (slots[1], far_b0, near[0], *shared, own_theirs[0])
    )
    slots.append(around(slots[1]))
    near.append(to_pair(slots[1]))
    pair_gate, pair_up = to_pair(shared[0]), to_pair(shared[1])
    far_own = to_across(far_own)
    pair_gate, pair_up, near[1] = lax.optimization_barrier((pair_gate, pair_up, near[1]))
    near_theirs = factors(at, pair_gate, pair_up, block, -2)

    slots[2], far_near, gate, pair_gate, section_layers = lax.optimization_barrier(
        (slots[2], near_theirs[0], gate, pair_gate, section_layers)
    )
    scale = section_scale(section_layers).reshape(1)
    norm = scale / jnp.sqrt(jnp.float32(rows * 4))
    slots.append(around(slots[2]))
    near.append(to_pair(slots[2]))
    cross_b = [to_pair(after(far_b0, slots[2]))]
    far_near = to_across(far_near)
    own_mine = factors(at, gate, up, block, 3)
    near_mine = factors(at, pair_gate, pair_up, block, -1)
    part = assemble(at, slots[:3], split)

    slots[3], near[2], cross_b[0], far_own, part, scale, norm, _, _ = lax.optimization_barrier(
        (slots[3], near[2], cross_b[0], far_own, part, scale, norm, own_mine[0], near_mine[0])
    )
    near.append(to_pair(slots[3]))
    piece = slots[3].shape[0]
    part = lax.dynamic_update_slice(part, slots[3][:, :split], (lax.rem(place + 1, 4) * piece, 0))
    far_a = to_across(part)
    far_b = [far_b0] + [around(after(far_b0, slots[3]), places) for places in (1, 2, 3)]

    own_gate, own_up, near_gate, near_up, rows_here = hidden_grad(
        at, scale, [*slots, *near], weight,
        [own_mine[1:], own_theirs[1:], near_mine[1:], near_theirs[1:]], 0, block,
    )
    near_gate, near_up, far_near, far_a, *far_b = lax.optimization_barrier(
        (near_gate, near_up, far_near, far_a, *far_b)
    )
    cross_a = to_pair(far_a)
    cross_b += [to_pair(slot) for slot in far_b[1:]]
    near_gate, near_up, cross_a, *cross_b = lax.optimization_barrier(
        (near_gate, near_up, cross_a, *cross_b)
    )
    from_pair = [to_pair(near_gate), to_pair(near_up)]

    hidden = [own_mine[0], near_mine[0], far_own, far_near]
    grad_gate, grad_up, grad_down_w = weight_grad(
        at, norm, hidden, rows_here, [far_a, cross_a], [*far_b, *cross_b], [own_gate, own_up]
    )
    for i, owner in enumerate((pair_mine, pair_theirs)):
        grad_gate = lax.dynamic_update_slice(grad_gate, from_pair[0][i], (0, owner * block))
        grad_up = lax.dynamic_update_slice(grad_up, from_pair[1][i], (0, owner * block))
    return (grad_gate[None, None], grad_up[None, None], grad_down_w[None])


def solution(mesh):
    def per_device(section_layers, grad_out, gate_act, up_act, down_weight):
        sizes = (grad_out.shape[2] % 16, gate_act.shape[3] % 1024, grad_out.shape[3] % 1024)
        small = mesh.shape["tensor"] == 4 and mesh.shape["dp"] == 4
        form = paired if small and sizes == (0, 0, 0) else general
        return form(section_layers, grad_out, gate_act, up_act, down_weight)

    placed = (
        P(),
        P("pipe", "dp", "tensor", None),
        P("pipe", "dp", None, "tensor"),
        P("pipe", "dp", None, "tensor"),
        P("pipe", "tensor", None),
    )
    return jax.shard_map(
        per_device,
        mesh=mesh,
        in_specs=placed,
        out_specs=(
            P("pipe", "dp", None, "tensor"),
            P("pipe", "dp", None, "tensor"),
            P("pipe", ("tensor", "dp"), None),
        ),
        check_vma=False,
    )
```
